512 devices in a mesh: dp: 64 (over z, x, core), head: 8 (over y).
Axes of the slice: x: 4, y: 8, z: 8, core: 2. Of those that a mesh axis runs over, the one named last changes fastest.
Arguments:
- queries: bfloat16 [8192, 4096], P('dp', 'head'), may hold values from -24 to 24
- keys: bfloat16 [8192, 1024], P('dp', 'head'), may hold values from -6 to 6
- values: bfloat16 [8192, 1024], P('dp', 'head'), may hold values from -6 to 6
- grad_logp: bfloat16 [8192, 4096], P('dp', 'head'), may hold values from -6 to 6
- policy_logp: float32 [8192], P(('dp', 'head')), may hold values from -1.5 to -0.1
- ref_logp: float32 [8192], P(('dp', 'head')), may hold values from -1.5 to -0.1
- resp_mask: int32 [8192], P(('dp', 'head')), may hold values 0 or 1
- seg_ids: int32 [8192], P('dp'), may hold values from 0 to 3, never falling along the last dimension, each value on 1 to 4096 neighbouring positions
Outputs:
- grad_queries: bfloat16 [8192, 4096], P('dp', 'head')
- grad_keys: bfloat16 [8192, 1024], P('dp', 'head')
- grad_values: bfloat16 [8192, 1024], P('dp', 'head')
The draws below stay inside these ranges and needn't reach their ends.
All inputs are finite; a program needn't handle non-finite values. No bound on the sum of `resp_mask` on one device may be relied on, other than what follows from the above.
Results may differ from the reference program's by a relative error of at most 0.0065.
Values may be sent and summed in bfloat16 or wider, within the bound.
A program may use at most 64 MiB of HBM per device.

```python
import math
import jax
import jax.numpy as jnp
import numpy as np
from jax import lax

HD = 128
QH_DEV = 4
SEGS = 4
KVH = 8
HEADS = 32
TOKENS = 8192
MOST = 4096
N_HEAD = 8


def draw_keys(key, part):
    key = jax.random.fold_in(key, 1)
    normal_base = jax.random.truncated_normal(key, -6.0, 6.0, (TOKENS, N_HEAD * HD), jnp.float32)
    return normal_base.astype(jnp.bfloat16)


def draw_queries(key, part):
    key = jax.random.fold_in(key, 2)
    normal_base = jax.random.truncated_normal(key, -6.0, 6.0, (TOKENS, N_HEAD * QH_DEV * HD), jnp.float32)
    return normal_base.astype(jnp.bfloat16)


def with_ends(entries, key, least, high):
    shape = entries.shape
    place = [jax.random.randint(jax.random.fold_in(key, axis), (), 0, shape[axis]) for axis in range(len(shape))]
    entries = entries.at[tuple(place)].set(least)
    longest = shape.index(max(shape))
    place[longest] = (place[longest] + 1) % shape[longest]
    return entries.at[tuple(place)].set(high)


def block_scale(rng, shape, pieces, least, high):
    level = 1.0
    for axis_at, parts in pieces:
        heights = jax.random.uniform(jax.random.fold_in(jax.random.fold_in(rng, 6), axis_at), (parts,), jnp.float32, least / len(pieces), high / len(pieces))
        level = level * jnp.repeat(jnp.exp(heights), shape[axis_at] // parts).reshape((-1,) + (1,) * (len(shape) - 1 - axis_at))
    return level


def profile(count, total, bound, skew):
    portions = [(1 << 20) // math.isqrt(rank ** skew) + 1 for rank in range(2, count + 1)]
    surplus, given = total - bound - (count - 1), [1] * (count - 1)
    while surplus > 0:
        movable = [i for i in range(count - 1) if given[i] < bound]
        mass, remaining = sum([portions[i] for i in movable]), surplus
        for i in movable:
            addition = min(bound - given[i], max(1, remaining * portions[i] // mass), surplus)
            given[i] = given[i] + addition
            surplus = surplus - addition
    return np.array([bound] + given)


def uneven_parts(stream_key, number_of, total, limit, skew):
    if number_of == 2:
        one = jax.random.randint(stream_key, (), max(1, total - limit), min(limit, total - 1) + 1)
        return jnp.stack([one, total - one])
    sizes = jnp.asarray(profile(number_of, total, limit, skew), jnp.int32)
    couples = (number_of - 1) // 2
    source_of, receiver = sizes[1:1 + 2 * couples:2], sizes[2:2 + 2 * couples:2]
    margin = jnp.minimum(source_of - 1, limit - receiver)
    passed = jax.random.randint(jax.random.fold_in(stream_key, 1), (couples,), 0, 1 << 20) % (margin + 1)
    sizes = sizes.at[1:1 + 2 * couples:2].set(source_of - passed).at[2:2 + 2 * couples:2].set(receiver + passed)
    return sizes[jax.random.permutation(jax.random.fold_in(stream_key, 2), number_of)]


def noise(rng, extent, width, reach, split=(), held_as=jnp.bfloat16):
    drawn = jax.random.normal(rng, extent, jnp.float32) * width
    if len(split) > 0:
        drawn = block_scale(rng, extent, split, -0.22, 0.18) * drawn
    return jnp.clip(drawn, min=-reach, max=reach).astype(held_as)


def setup_inputs(seed: int = 0) -> dict:
    arg_keys = jax.random.split(jax.random.key(seed), 9)
    return {
        "queries": draw_queries(jax.random.fold_in(arg_keys[8], 71), 0),
        "keys": draw_keys(jax.random.fold_in(arg_keys[8], 71), 0),
        "values": noise(arg_keys[2], (TOKENS, KVH * HD), 1.0, 6.0, ((0, 64), (1, 8))),
        "grad_logp": noise(arg_keys[3], (TOKENS, HEADS * HD), 1.0, 6.0, ((0, 64), (1, 8))),
        "policy_logp": jnp.clip(-1.5 + 1.4 * jax.random.uniform(arg_keys[4], (TOKENS,), jnp.float32) ** block_scale(arg_keys[4], (TOKENS,), ((0, 512),), -0.2, 0.2), -1.5, -0.1),
        "ref_logp": jnp.clip(-1.5 + 1.4 * jax.random.uniform(arg_keys[5], (TOKENS,), jnp.float32) ** block_scale(arg_keys[5], (TOKENS,), ((0, 512),), -0.2, 0.2), -1.5, -0.1),
        "resp_mask": with_ends((jax.random.randint(arg_keys[6], (TOKENS,), 0, 3) < 2).astype(jnp.int32), jax.random.fold_in(arg_keys[6], 1), 0, 1),
        "seg_ids": jnp.searchsorted(jnp.cumsum(uneven_parts(arg_keys[7], SEGS, TOKENS, MOST, 0)), jnp.arange(TOKENS), side="right").astype(jnp.int32),
    }


def reference(queries, keys, values, grad_logp, policy_logp, ref_logp, resp_mask, seg_ids):
    tokens = queries.shape[0]
    score_scale = HD ** -0.5
    weights = resp_mask.astype(jnp.float32)
    member = (seg_ids[:, None] == jnp.arange(SEGS)[None, :]).astype(jnp.float32)
    counts = jnp.sum(member * weights[:, None], 0)
    denominator = jnp.maximum(jnp.sum(member * counts[None, :], 1), 1.0)
    token_weight = (1.0 - jnp.exp(ref_logp - policy_logp)) * weights * (tokens / SEGS) / denominator
    grad_out = (token_weight[:, None] * grad_logp.astype(jnp.float32)).astype(jnp.bfloat16)
    group_count = N_HEAD
    query_groups = queries.reshape(tokens, group_count, QH_DEV, HD).transpose(1, 0, 2, 3)
    out_groups = grad_out.reshape(tokens, group_count, QH_DEV, HD).transpose(1, 0, 2, 3)
    key_groups = keys.reshape(tokens, group_count, HD).transpose(1, 0, 2)
    value_groups = values.reshape(tokens, group_count, HD).transpose(1, 0, 2)
    positions = jnp.arange(tokens)
    block_rows = min(512, tokens)
    block_count = tokens // block_rows

    def one_group(operands):
        query_one, out_one, key_one, value_one = operands
        keys_wide = key_one.astype(jnp.float32)
        values_wide = value_one.astype(jnp.float32)

        def block_work(state_carry, block_index):
            dk_sum, dv_sum = state_carry
            row_start = block_index * block_rows
            query_block = lax.dynamic_slice_in_dim(query_one, row_start, block_rows).astype(jnp.float32)
            out_block = lax.dynamic_slice_in_dim(out_one, row_start, block_rows).astype(jnp.float32)
            query_pos = row_start + jnp.arange(block_rows)
            query_seg = lax.dynamic_slice_in_dim(seg_ids, row_start, block_rows)
            allowed = (positions[None, :] <= query_pos[:, None]) & (seg_ids[None, :] == query_seg[:, None])
            live_mask = allowed[None]
            scores = jnp.einsum('thd,sd->hts', query_block, keys_wide) * score_scale
            grad_prob = jnp.einsum('thd,sd->hts', out_block, values_wide)
            row_top = jnp.max(jnp.where(live_mask, scores, -1e30), -1)
            weighted = jnp.where(live_mask, jnp.exp(scores - row_top[..., None]), 0.0)
            log_total = row_top + jnp.log(jnp.sum(weighted, -1))
            softmax_prob = jnp.where(live_mask, jnp.exp(scores - log_total[..., None]), 0.0)
            row_delta = jnp.sum(softmax_prob * grad_prob, -1)
            prob_low = lax.optimization_barrier(softmax_prob.astype(jnp.bfloat16)).astype(jnp.float32)
            grad_score = lax.optimization_barrier(
                (softmax_prob * (grad_prob - row_delta[..., None])).astype(jnp.bfloat16)).astype(jnp.float32)
            dv_sum = dv_sum + jnp.einsum('hts,thd->sd', prob_low, out_block)
            dk_sum = dk_sum + jnp.einsum('hts,thd->sd', grad_score, query_block)
            dq_block = (jnp.einsum('hts,sd->thd', grad_score, keys_wide) * score_scale).astype(jnp.bfloat16)
            return (dk_sum, dv_sum), dq_block

        zeros_init = (jnp.zeros((tokens, HD), jnp.float32), jnp.zeros((tokens, HD), jnp.float32))
        (dk_sum, dv_sum), dq_blocks = lax.scan(block_work, zeros_init, jnp.arange(block_count).astype(jnp.int32))
        dq_group = dq_blocks.reshape(tokens, QH_DEV, HD)
        return dq_group, (dk_sum * score_scale).astype(jnp.bfloat16), dv_sum.astype(jnp.bfloat16)

    dq_all, dk_all, dv_all = lax.map(one_group, (query_groups, out_groups, key_groups, value_groups))
    grad_queries = dq_all.transpose(1, 0, 2, 3).reshape(tokens, group_count * QH_DEV * HD)
    grad_keys = dk_all.transpose(1, 0, 2).reshape(tokens, group_count * HD)
    grad_values = dv_all.transpose(1, 0, 2).reshape(tokens, group_count * HD)
    return (grad_queries, grad_keys, grad_values)
```

```python
import functools
import math

import jax
import jax.numpy as jnp
from jax import lax
from jax.experimental import pallas as pl
from jax.experimental.pallas import tpu as pltpu
from jax.sharding import PartitionSpec as P

HD = 128
QH = 4
SEGS = 4
MOST = 4096
XN = 4
CORES = 2
NP = XN * CORES
TOK = 128
ROWS = QH * TOK
PLANE = NP * TOK
ND = MOST // PLANE
SCALE = HD ** -0.5
C2 = SCALE * math.log2(math.e)
NEG = -1e30
MESH = pl.DeviceIdType.MESH
F32 = jnp.float32
BF = jnp.bfloat16
OFFS = (0, -1, 1, 2)
OFF_AT = {0: 0, 3: 1, 1: 2, 2: 3}
BACK = (0, 2, 1, 3)


def dot_nt(a, b):
    return lax.dot_general(a, b, (((1,), (1,)), ((), ())), preferred_element_type=F32)


def dot_nn(a, b):
    return lax.dot_general(a, b, (((1,), (0,)), ((), ())), preferred_element_type=F32)


def kernel(
    zn, yn, q_ref, g_ref, k_ref, v_ref, small_ref, dq_ref, dk_ref, dv_ref,
    qb, gb, ob, kv, kt, pky, pkp, pkz, lob, wb, db, skb, stl, stx, rdb,
    acc, dqt, dqp, dqs, dqr, cs, cr,
    loc, sq, rq, rg, ksend, krecv, ysend, yrecv, psend, precv, zsend, zrecv,
    tsend, trecv, pxs, pxr, dss, dsr, css, crs,
):
    dp = lax.axis_index("dp")
    head = lax.axis_index("head")
    z = dp // NP
    p_own = dp % NP
    x = p_own // CORES
    core = p_own % CORES

    def plane_dev(i, b):
        xx = (x + (OFFS[i] + XN)) % XN
        return {"dp": z * NP + xx * CORES + (core + b) % CORES}

    def z_dev(o):
        return {"dp": ((z + o) % zn) * NP + p_own}

    def y_dev(o):
        return {"head": (head + o) % yn}

    others = [(i, b) for i in range(XN) for b in range(CORES) if (i, b) != (0, 0)]
    sends = []

    def push(src, dst, ssem, rsem, dev):
        copy = pltpu.make_async_remote_copy(
            src_ref=src, dst_ref=dst, send_sem=ssem, recv_sem=rsem,
            device_id=dev, device_id_type=MESH,
        )
        copy.start()
        sends.append(copy)
        return copy

    barrier = pltpu.get_barrier_semaphore()
    partners = [plane_dev(i, b) for i, b in others]
    partners += [z_dev(o) for o in range(1, zn)] + [y_dev(o) for o in range(1, yn)]
    for dev in partners:
        pl.semaphore_signal(barrier, inc=1, device_id=dev, device_id_type=MESH)
    pl.semaphore_wait(barrier, len(partners))

    kv_copies = {}
    for n, ref in ((0, k_ref), (1, v_ref)):
        kv_copies[1, n] = push(ref, kv.at[1, n], ksend.at[0, n], krecv.at[1, n], z_dev(1))
    q_copies, g_copies = {}, {}
    q_copies[4] = None
    q_copies[2] = push(q_ref, qb.at[2], sq.at[0], rq.at[2], plane_dev(2, 0))
    g_copies[4] = push(g_ref, gb.at[4], sq.at[1], rg.at[4], plane_dev(1, 0))
    g_copies[2] = push(g_ref, gb.at[2], sq.at[2], rg.at[2], plane_dev(2, 0))
    q_copies[4] = push(q_ref, qb.at[4], sq.at[3], rq.at[4], plane_dev(1, 0))
    q_copies[1] = push(q_ref, qb.at[1], sq.at[4], rq.at[1], plane_dev(0, 1))
    g_copies[1] = push(g_ref, gb.at[1], sq.at[5], rg.at[1], plane_dev(0, 1))
    local = [
        pltpu.make_async_copy(q_ref, qb.at[0], loc.at[0]),
        pltpu.make_async_copy(g_ref, gb.at[0], loc.at[1]),
        pltpu.make_async_copy(k_ref, kv.at[0, 0], loc.at[2]),
        pltpu.make_async_copy(v_ref, kv.at[0, 1], loc.at[3]),
    ]
    for copy in local:
        copy.start()

    lane = lax.broadcasted_iota(jnp.int32, (1, TOK), 1)
    part = TOK // yn
    mine = (lane >= head * part) & (lane < (head + 1) * part)
    mask_row = jnp.where(mine, small_ref[2:3, :], 0.0)
    num_row = (1.0 - jnp.exp(small_ref[1:2, :] - small_ref[0:1, :])) * mask_row
    pky[0] = jnp.concatenate([num_row, mask_row, jnp.zeros((6, TOK), F32)], axis=0)
    y_copies = [
        push(pky.at[0], pky.at[o], ysend.at[o - 1], yrecv.at[o - 1], y_dev(o))
        for o in range(1, yn)
    ]
    for copy in local:
        copy.wait()
    kt[0] = kv[0, 0].astype(F32).T.astype(BF)
    for copy in y_copies:
        copy.wait_recv()
    total = pky[0]
    for o in range(1, yn):
        total = total + pky[o]
    seg_row = small_ref[3:4, :]
    pkp[0] = jnp.concatenate([total[0:2], seg_row, jnp.zeros((5, TOK), F32)], axis=0)
    p_copies = [
        push(pkp.at[0], pkp.at[2 * BACK[i] + b], psend.at[n], precv.at[n], plane_dev(i, b))
        for n, (i, b) in enumerate(others)
    ]

    def forward_kv(d):
        for n in (0, 1):
            kv_copies[d, n].wait_recv()
            if d < ND:
                kv_copies[d + 1, n] = push(
                    kv.at[d, n], kv.at[d + 1, n], ksend.at[d, n], krecv.at[d + 1, n], z_dev(1)
                )
        kt[d] = kv[d, 0].astype(F32).T.astype(BF)

    forward_kv(1)
    for copy in p_copies:
        copy.wait_recv()
    cnt = [jnp.zeros((1, TOK), F32) for _ in range(SEGS)]
    size = [jnp.zeros((1, TOK), F32) for _ in range(SEGS)]
    for n in range(NP):
        m_row, s_row = pkp[n, 1:2, :], pkp[n, 2:3, :]
        for s in range(SEGS):
            here = s_row == float(s)
            cnt[s] = cnt[s] + jnp.where(here, m_row, 0.0)
            size[s] = size[s] + jnp.where(here, 1.0, 0.0)
    pkz[0] = jnp.concatenate(cnt + size, axis=0)
    z_copies = [
        push(pkz.at[0], pkz.at[o], zsend.at[o - 1], zrecv.at[o - 1], z_dev(o))
        for o in range(1, zn)
    ]
    q_copies[2].wait_recv()
    q_copies[6] = push(qb.at[2], qb.at[6], sq.at[6], rq.at[6], plane_dev(2, 0))
    q_copies[3] = push(qb.at[2], qb.at[3], sq.at[7], rq.at[3], plane_dev(0, 1))
    g_copies[4].wait_recv()
    g_copies[6] = push(gb.at[4], gb.at[6], sq.at[8], rg.at[6], plane_dev(1, 0))
    g_copies[5] = push(gb.at[4], gb.at[5], sq.at[9], rg.at[5], plane_dev(0, 1))
    for copy in z_copies:
        copy.wait_recv()
    total = pkz[0]
    for o in range(1, zn):
        total = total + pkz[o]
    total = jnp.sum(total, axis=1, keepdims=True)
    starts = [jnp.zeros((1, 1), F32)]
    for s in range(SEGS - 1):
        starts.append(starts[-1] + total[SEGS + s:SEGS + s + 1])
    zero = (z * PLANE).astype(F32)
    tokens = float(zn * PLANE)

    def prepare(s):
        num, seg = pkp[s, 0:1, :], pkp[s, 2:3, :]
        count = jnp.zeros((1, TOK), F32)
        begin = jnp.zeros((1, TOK), F32)
        for n in range(SEGS):
            here = seg == float(n)
            count = jnp.where(here, total[n:n + 1], count)
            begin = jnp.where(here, starts[n], begin)
        weight = num * (tokens / SEGS) / jnp.maximum(count, 1.0)
        row = lax.broadcasted_iota(jnp.int32, (TOK, TOK), 0)
        col = lax.broadcasted_iota(jnp.int32, (TOK, TOK), 1)
        weight_col = jnp.sum(jnp.where(row == col, weight, 0.0), axis=1, keepdims=True)
        for h in range(QH):
            cols = slice(h * HD, (h + 1) * HD)
            ob[s, cols, :] = (weight_col * gb[s, :, cols].astype(F32)).astype(BF)
        begin = (begin - zero).astype(jnp.int32)
        lob[s, 0:1, :] = jnp.concatenate([begin] * QH, axis=1)

    def q_rows(s, first, count):
        return jnp.concatenate(
            [qb[s, :, h * HD:(h + 1) * HD] for h in range(first, first + count)], axis=0
        )

    STEP = 2

    def tile1(s, d, at, causal):
        base = p_own * TOK - d * PLANE
        width = STEP * TOK
        for first in range(0, QH, STEP):
            cols = slice(first * TOK, (first + STEP) * TOK)
            scores = dot_nt(kv[d, 0], q_rows(s, first, STEP))
            cross = dot_nt(kv[d, 1], ob[s, cols, :])
            key_pos = lax.broadcasted_iota(jnp.int32, (TOK, width), 0) + base
            ok = key_pos >= lob[s, 0:1, cols]
            if causal:
                q_pos = lax.broadcasted_iota(jnp.int32, (TOK, width), 1) % TOK + p_own * TOK
                ok = ok & (key_pos <= q_pos)
            scores = jnp.where(ok, scores, NEG)
            top = jnp.max(scores, axis=0, keepdims=True)
            w = jnp.exp2((scores - top) * C2)
            wb[at, :, cols] = w
            db[at, :, cols] = cross
            skb[at, 0:1, cols] = top
            skb[at, 1:2, cols] = jnp.sum(w, axis=0, keepdims=True)
            skb[at, 2:3, cols] = jnp.sum(w * cross, axis=0, keepdims=True)

    def slot_p(s):
        i, b = s // CORES, s % CORES
        off = jnp.where(i == 1, XN - 1, jnp.where(i == 2, 1, jnp.where(i == 3, 2, 0)))
        return ((x + off) % XN) * CORES + (core + b) % CORES

    def far_d(s):
        return jnp.where(slot_p(s) > p_own, 0, ND)

    t_copies = []

    def send_stats(i):
        for b in range(CORES):
            s = 2 * i + b
            ats = [s * ND + n for n in range(ND)] + ([NP * ND] if s == 0 else [])
            top = skb[ats[0], 0:1, :]
            for at in ats[1:]:
                top = jnp.maximum(top, skb[at, 0:1, :])
            mass = jnp.zeros((1, ROWS), F32)
            mix = jnp.zeros((1, ROWS), F32)
            for at in ats:
                f = jnp.exp2((skb[at, 0:1, :] - top) * C2)
                mass = mass + f * skb[at, 1:2, :]
                mix = mix + f * skb[at, 2:3, :]
            stl[i, 3 * b:3 * b + 1, :] = top
            stl[i, 3 * b + 1:3 * b + 2, :] = mass
            stl[i, 3 * b + 2:3 * b + 3, :] = mix
        for n, (j, b) in enumerate(others):
            t_copies.append(push(
                stl.at[i], stx.at[2 * BACK[j] + b, i], tsend.at[n, i],
                trecv.at[2 * BACK[j] + b, i], plane_dev(j, b),
            ))

    prepare(0)
    tile1(0, 0, NP * ND, True)
    q_copies[1].wait_recv()
    g_copies[1].wait_recv()
    prepare(1)

    def pair(i, d):
        def body(b, carry):
            s = 2 * i + b
            if d < ND:
                tile1(s, d, s * ND + d, False)
            else:
                tile1(s, far_d(s), s * ND, False)
            return carry

        lax.fori_loop(0, CORES, body, 0)

    pair(0, 1)
    forward_kv(2)
    pair(0, 2)
    forward_kv(3)
    pair(0, 3)
    g_copies[2].wait_recv()
    g_copies[7 - 4] = push(gb.at[2], gb.at[3], sq.at[10], rg.at[3], plane_dev(0, 1))
    q_copies[4].wait_recv()
    q_copies[5] = push(qb.at[4], qb.at[5], sq.at[11], rq.at[5], plane_dev(0, 1))
    forward_kv(4)
    pair(0, 4)
    send_stats(0)

    def whole(i):
        def body(n, carry):
            s = 2 * i + n // ND
            d = n % ND
            tile1(s, jnp.where(d == 0, far_d(s), d), s * ND + d, False)
            return carry

        lax.fori_loop(0, CORES * ND, body, 0)
        send_stats(i)

    for s in (2, 3):
        if s == 3:
            q_copies[s].wait_recv()
            g_copies[s].wait_recv()
        prepare(s)
    whole(1)
    q_copies[6].wait_recv()
    q_copies[7] = push(qb.at[6], qb.at[7], sq.at[12], rq.at[7], plane_dev(0, 1))
    g_copies[6].wait_recv()
    g_copies[7] = push(gb.at[6], gb.at[7], sq.at[13], rg.at[7], plane_dev(0, 1))
    for s in (4, 5):
        if s == 5:
            q_copies[s].wait_recv()
            g_copies[s].wait_recv()
        prepare(s)
    whole(2)
    prepare(6)
    q_copies[7].wait_recv()
    g_copies[7].wait_recv()
    prepare(7)
    whole(3)
    for d in range(ND + 1):
        acc[d] = jnp.zeros((2, TOK, HD), F32)
    for copy in t_copies:
        copy.wait_recv()

    for i in range(XN):
        for b in range(CORES):
            s = 2 * i + b
            found = []
            for j in range(XN):
                for a in range(CORES):
                    at = OFF_AT[(OFFS[i] - OFFS[j]) % XN]
                    r = 3 * (b ^ a)
                    src = stl.at[at] if (j, a) == (0, 0) else stx.at[2 * j + a, at]
                    found.append((src[r:r + 1, :], src[r + 1:r + 2, :], src[r + 2:r + 3, :]))
            top = found[0][0]
            for f in found[1:]:
                top = jnp.maximum(top, f[0])
            mass = jnp.zeros((1, ROWS), F32)
            mix = jnp.zeros((1, ROWS), F32)
            for f in found:
                e = jnp.exp2((f[0] - top) * C2)
                mass = mass + e * f[1]
                mix = mix + e * f[2]
            inv = 1.0 / mass
            rdb[s, 0:1, :] = mix * inv
            for at in [s * ND + n for n in range(ND)] + ([NP * ND] if s == 0 else []):
                skb[at, 3:4, :] = jnp.exp2((skb[at, 0:1, :] - top) * C2) * inv

    def tile2(s, d, at):
        prob = wb[at] * skb[at, 3:4, :]
        low = prob.astype(BF)
        score = (prob * (db[at] - rdb[s, 0:1, :])).astype(BF)
        acc[d, 1] = acc[d, 1] + dot_nn(low, ob[s])
        acc[d, 0] = acc[d, 0] + dot_nn(score, q_rows(s, 0, QH))
        return dot_nn(kt[d], score)

    def slot2(s):
        far = far_d(s)
        total = tile2(s, far, s * ND)
        for d in range(1, ND):
            total = total + tile2(s, d, s * ND + d)
        dqt[s] = total

    def to_partner(i):
        return pltpu.make_async_remote_copy(
            src_ref=dqt.at[2 * i + 1], dst_ref=dqp.at[i], send_sem=pxs.at[i],
            recv_sem=pxr.at[i], device_id=plane_dev(0, 1), device_id_type=MESH,
        )

    d_copies = []
    for i in (3, 1, 2, 0):
        def body(n, carry):
            slot2(2 * i + 1 - n)
            return carry

        slot2(2 * i + 1)
        copy = to_partner(i)
        copy.start()
        sends.append(copy)
        slot2(2 * i)
        if i > 0:
            copy.wait_recv()
            dqs[i - 1] = (dqt[2 * i] + dqp[i]).astype(BF)
            d_copies.append(push(
                dqs.at[i - 1], dqr.at[BACK[i] - 1], dss.at[i - 1], dsr.at[BACK[i] - 1],
                plane_dev(i, 0),
            ))
        else:
            own = copy
    dqt[0] = dqt[0] + tile2(0, 0, NP * ND)

    c_copies = {}
    for n in (0, 1):
        cs[0, n] = acc[ND, n].astype(BF)
        c_copies[0, n] = push(cs.at[0, n], cr.at[0, n], css.at[0, n], crs.at[0, n], z_dev(zn - 1))
    for step in range(1, ND):
        for n in (0, 1):
            c_copies[step - 1, n].wait_recv()
            cs[step, n] = (acc[ND - step, n] + cr[step - 1, n].astype(F32)).astype(BF)
            c_copies[step, n] = push(
                cs.at[step, n], cr.at[step, n], css.at[step, n], crs.at[step, n], z_dev(zn - 1)
            )
    own.wait_recv()
    for copy in d_copies:
        copy.wait_recv()
    total = dqt[0] + dqp[0]
    for i in range(XN - 1):
        total = total + dqr[i].astype(F32)
    total = total * SCALE
    for h in range(QH):
        cols = slice(h * HD, (h + 1) * HD)
        dq_ref[:, cols] = total[:, cols].T.astype(BF)
    for n in (0, 1):
        c_copies[ND - 1, n].wait_recv()
    dk_ref[...] = ((acc[0, 0] + cr[ND - 1, 0].astype(F32)) * SCALE).astype(BF)
    dv_ref[...] = (acc[0, 1] + cr[ND - 1, 1].astype(F32)).astype(BF)
    for copy in sends:
        copy.wait_send()


def per_device(zn, yn, queries, keys, values, grad_logp, policy_logp, ref_logp, resp_mask, seg_ids):
    rows = [policy_logp, ref_logp, resp_mask.astype(F32)]
    rows = [jnp.tile(r, yn)[None] for r in rows] + [seg_ids.astype(F32)[None]]
    small = jnp.concatenate(rows + [jnp.zeros((4, TOK), F32)], axis=0)
    dma = pltpu.SemaphoreType.DMA
    anyspace = pl.BlockSpec(memory_space=pl.ANY)
    vmem = pl.BlockSpec(memory_space=pltpu.VMEM)
    tiles = NP * ND + 1
    scratch = [
        pltpu.VMEM((NP, TOK, ROWS), BF),
        pltpu.VMEM((NP, TOK, ROWS), BF),
        pltpu.VMEM((NP, ROWS, HD), BF),
        pltpu.VMEM((ND + 1, 2, TOK, HD), BF),
        pltpu.VMEM((ND + 1, HD, TOK), BF),
        pltpu.VMEM((yn, 8, TOK), F32),
        pltpu.VMEM((NP, 8, TOK), F32),
        pltpu.VMEM((zn, 8, TOK), F32),
        pltpu.VMEM((NP, 8, ROWS), jnp.int32),
        pltpu.VMEM((tiles, TOK, ROWS), F32),
        pltpu.VMEM((tiles, TOK, ROWS), F32),
        pltpu.VMEM((tiles, 8, ROWS), F32),
        pltpu.VMEM((XN, 8, ROWS), F32),
        pltpu.VMEM((NP, XN, 8, ROWS), F32),
        pltpu.VMEM((NP, 8, ROWS), F32),
        pltpu.VMEM((ND + 1, 2, TOK, HD), F32),
        pltpu.VMEM((NP, HD, ROWS), F32),
        pltpu.VMEM((XN, HD, ROWS), F32),
        pltpu.VMEM((XN - 1, HD, ROWS), BF),
        pltpu.VMEM((XN - 1, HD, ROWS), BF),
        pltpu.VMEM((ND, 2, TOK, HD), BF),
        pltpu.VMEM((ND, 2, TOK, HD), BF),
        dma((4,)), dma((14,)), dma((NP,)), dma((NP,)),
        dma((ND, 2)), dma((ND + 1, 2)),
        dma((yn,)), dma((yn,)), dma((NP,)), dma((NP,)), dma((zn,)), dma((zn,)),
        dma((NP, XN)), dma((NP, XN)), dma((XN,)), dma((XN,)),
        dma((XN,)), dma((XN,)), dma((ND, 2)), dma((ND, 2)),
    ]
    return pl.pallas_call(
        functools.partial(kernel, zn, yn),
        out_shape=(
            jax.ShapeDtypeStruct((TOK, ROWS), BF),
            jax.ShapeDtypeStruct((TOK, HD), BF),
            jax.ShapeDtypeStruct((TOK, HD), BF),
        ),
        in_specs=[anyspace] * 4 + [vmem],
        out_specs=(vmem, vmem, vmem),
        scratch_shapes=scratch,
        compiler_params=pltpu.CompilerParams(
            collective_id=0, has_side_effects=True, vmem_limit_bytes=56 * 1024 * 1024
        ),
    )(queries, grad_logp, keys, values, small)


def solution(mesh):
    both, one = P("dp", "head"), P(("dp", "head"))
    return jax.shard_map(
        functools.partial(per_device, mesh.shape["dp"] // NP, mesh.shape["head"]),
        mesh=mesh,
        in_specs=(both,) * 4 + (one,) * 3 + (P("dp"),),
        out_specs=(both,) * 3,
        check_vma=False,
    )
```
